256 devices in a mesh: pipe: 8 (over x, y_hi), ctx: 32 (over y_lo, z, core).
Axes of the slice: x: 4, y: 4 (y_hi: 2, y_lo: 2; y = y_hi * 2 + y_lo), z: 8, core: 2. Of those that a mesh axis runs over, the one named last changes fastest.
Arguments:
- stored_acts: bfloat16 [8, 4096, 1024], P('pipe', 'ctx'), may hold values from -6 to 6
- queries: bfloat16 [8, 4096, 1024], P('pipe', 'ctx'), may hold values from -40 to 40
- patch_times: int32 [8, 4096], P('pipe', 'ctx'), may hold values from 0 to 31, as said below
- key_gain: float32 [8, 1024], P('pipe'), may hold values from 0.5 to 2
- value_gain: float32 [8, 1024], P('pipe'), may hold values from 0.5 to 2
- conv_weight: bfloat16 [8, 27, 128, 128], P('pipe'), may hold values from -0.109375 to 0.109375
- prior_grad: bfloat16 [8, 4096, 1024], P('pipe', 'ctx'), may hold values from -6 to 6
- loss_grad: bfloat16 [4096, 1024], P('ctx'), may hold values from -6 to 6
Outputs:
- input_grad: bfloat16 [8, 4096, 1024], P('pipe', 'ctx')
The draws below stay inside these ranges and needn't reach their ends.
Inputs may be any that keep to these rules, and one draw needn't show every extreme that they name: `patch_times`: within each aligned group of four patches of a sequence, no patch has a later time step than the first of the group.
All inputs are finite; a program needn't handle non-finite values.
Results may differ from the reference program's by a relative error of at most 0.012.
Values may be sent and summed in bfloat16 or wider, within the bound.
No kernel may reach another device: no remote copies, remote signals or barrier semaphores. Data moves between devices by JAX's collectives and lax.ppermute only.
A program may use at most 128 MiB of HBM per device.

```python
import math
import jax
import jax.numpy as jnp
from jax import lax

HEADS = 16
HEAD_DIM = 64
CHANNELS = 128
GY = 8
GZ = 8
TSTEPS = 32
D = 1024
FIELDS = 8
TOKENS = 4096
SECTIONS = 8


def acts_field(key):
    array_shape = (SECTIONS, TOKENS // 4, 4, D)
    values_base = jnp.clip(jax.random.normal(jax.random.fold_in(key, 11), array_shape, jnp.float32), -6.0, 6.0)
    return values_base.reshape(SECTIONS, TOKENS, D)


def draw_stored_acts(key, part):
    return acts_field(key).astype(jnp.bfloat16)


def draw_queries(key, part):
    array_shape = (SECTIONS, TOKENS, D)
    values_base = 2.0 * jnp.clip(jax.random.normal(jax.random.fold_in(key, 21), array_shape, jnp.float32), -6.0, 6.0)
    return values_base.astype(jnp.bfloat16)


def draw_patch_times(key, part):
    first_row = jax.random.randint(jax.random.fold_in(key, 31), (SECTIONS, TOKENS // 4, 1), 0, TSTEPS)
    later_rows = jax.random.randint(jax.random.fold_in(key, 32), (SECTIONS, TOKENS // 4, 3), 0, first_row + 1)
    return jnp.concatenate([first_row, later_rows], axis=2).reshape(SECTIONS, TOKENS).astype(jnp.int32)


def shard_levels(stream_key, extent, pieces, least, high):
    loudness, own = 1.0, jax.random.fold_in(stream_key, 6)
    for dim, shards_of in pieces:
        heights = jnp.exp(jax.random.uniform(jax.random.fold_in(own, dim), (shards_of,), jnp.float32, least / len(pieces), high / len(pieces)))
        loudness = loudness * jnp.repeat(heights, extent[dim] // shards_of).reshape([-1 if axis == dim else 1 for axis in range(len(extent))])
    return loudness


def normal_values(rng, extent, spread, limit, pieces=(), kind=jnp.bfloat16):
    loudness = shard_levels(rng, extent, pieces, -0.22, 0.18) if pieces else 1.0
    array = jax.random.normal(rng, extent, jnp.float32) * spread * loudness
    return jnp.minimum(jnp.maximum(array, -limit), limit).astype(kind)


def setup_inputs(seed: int = 0) -> dict:
    keys = jax.random.split(jax.random.key(seed), 9)
    return {
        "stored_acts": draw_stored_acts(jax.random.fold_in(keys[8], 71), 0),
        "queries": draw_queries(jax.random.fold_in(keys[8], 71), 0),
        "patch_times": draw_patch_times(jax.random.fold_in(keys[8], 71), 0),
        "key_gain": jnp.clip(jnp.exp(math.log(2.0) - 1.3862944 * jax.random.uniform(keys[3], (SECTIONS, D), jnp.float32) ** shard_levels(keys[3], (SECTIONS, D), ((0, 8),), -0.2, 0.2)), 0.5, 2.0),
        "value_gain": jnp.clip(jnp.exp(math.log(2.0) - 1.3862944 * jax.random.uniform(keys[4], (SECTIONS, D), jnp.float32) ** shard_levels(keys[4], (SECTIONS, D), ((0, 8),), -0.2, 0.2)), 0.5, 2.0),
        "conv_weight": normal_values(keys[5], (SECTIONS, 27, CHANNELS, CHANNELS), (27 * CHANNELS) ** -0.5, 0.109375, ((0, 8),)),
        "prior_grad": normal_values(keys[6], (SECTIONS, TOKENS, D), 1.0, 6.0, ((0, 8), (1, 32))),
        "loss_grad": normal_values(keys[7], (TOKENS, D), 1.0, 6.0, ((0, 32),)),
    }


def conv_backward(gradient, weight):
    planes = gradient.shape[0] // (GY * GZ)
    grid_field = gradient.reshape(planes, GY, GZ, FIELDS, CHANNELS)
    padded = jnp.pad(grid_field, ((1, 1), (1, 1), (1, 1), (0, 0), (0, 0)))
    accumulated = jnp.zeros((planes * GY * GZ * FIELDS, CHANNELS), jnp.float32)
    for shift_x in (-1, 0, 1):
        for shift_y in (-1, 0, 1):
            for shift_z in (-1, 0, 1):
                offset = 9 * (shift_x + 1) + 3 * (shift_y + 1) + (shift_z + 1)
                window = padded[1 - shift_x:1 - shift_x + planes, 1 - shift_y:1 - shift_y + GY, 1 - shift_z:1 - shift_z + GZ]
                accumulated = accumulated + jnp.dot(window.reshape(-1, CHANNELS), weight[offset].T, preferred_element_type=jnp.float32)
    return accumulated.reshape(gradient.shape[0], D)


def section_gradient(section_items):
    acts_rows, query_rows, time_rows, key_scale, value_scale, incoming, weight = section_items
    length = acts_rows.shape[0]
    widened = acts_rows.astype(jnp.float32)
    keyed = (widened * key_scale).astype(jnp.bfloat16).reshape(length, HEADS, HEAD_DIM)
    valued = jnp.roll((widened * value_scale).astype(jnp.bfloat16).reshape(length, HEADS, HEAD_DIM), HEADS // 2, axis=1)
    query_heads = query_rows.reshape(length, HEADS, HEAD_DIM)
    grad_heads = incoming.reshape(length, HEADS, HEAD_DIM)
    block_size = math.gcd(length, 512)
    scale_factor = HEAD_DIM ** -0.5

    def per_head(head_items):
        head_query, head_grad, head_key, head_value = head_items

        def per_block(running, block_index):
            key_grad, value_grad = running
            first_row = (block_index * block_size).astype(jnp.int32)
            block_query = lax.dynamic_slice_in_dim(head_query, first_row, block_size, 0)
            block_grad = lax.dynamic_slice_in_dim(head_grad, first_row, block_size, 0)
            block_times = lax.dynamic_slice_in_dim(time_rows, first_row, block_size, 0)
            scores = jnp.dot(block_query, head_key.T, preferred_element_type=jnp.float32) * scale_factor
            scores = jnp.where(time_rows[None, :] <= block_times[:, None], scores, -jnp.inf)
            exponent = jnp.exp(scores - jnp.max(scores, axis=1, keepdims=True))
            probability = exponent / jnp.sum(exponent, axis=1, keepdims=True)
            prob_grad = jnp.dot(block_grad, head_value.T, preferred_element_type=jnp.float32)
            delta_rows = jnp.sum(probability * prob_grad, axis=1, keepdims=True)
            score_grad = (probability * (prob_grad - delta_rows)).astype(jnp.bfloat16)
            value_grad = value_grad + jnp.dot(probability.astype(jnp.bfloat16).T, block_grad, preferred_element_type=jnp.float32)
            key_grad = key_grad + jnp.dot(score_grad.T, block_query, preferred_element_type=jnp.float32) * scale_factor
            return (key_grad, value_grad), None

        empty = jnp.zeros((length, HEAD_DIM), jnp.float32)
        (key_grad, value_grad), _ = lax.scan(per_block, (empty, empty), jnp.arange(length // block_size, dtype=jnp.int32))
        return key_grad, value_grad

    key_grad, value_grad = lax.map(per_head, (query_heads.transpose(1, 0, 2), grad_heads.transpose(1, 0, 2), keyed.transpose(1, 0, 2), valued.transpose(1, 0, 2)))
    key_part = key_grad.transpose(1, 0, 2).reshape(length, D) * key_scale
    value_part = jnp.roll(value_grad.transpose(1, 0, 2), HEADS // 2, axis=1).reshape(length, D) * value_scale
    return (conv_backward(incoming, weight) + key_part + value_part).astype(jnp.bfloat16)


def reference(stored_acts, queries, patch_times, key_gain, value_gain, conv_weight, prior_grad, loss_grad):
    incoming = jnp.concatenate([prior_grad[1:], loss_grad[None]], axis=0)
    return lax.map(section_gradient, (stored_acts, queries, patch_times, key_gain, value_gain, incoming, conv_weight))
```

```python
import functools

import jax
import jax.numpy as jnp
from jax import lax
from jax.experimental import pallas as pl
from jax.experimental.pallas import tpu as pltpu
from jax.sharding import Mesh, PartitionSpec as P

HEADS = 16
HEAD_DIM = 64
CHANNELS = 128
GY = 8
GZ = 8
D = 1024
FIELDS = 8
ROWS = 128
PAIR = 128
RING = 8
TIMES = 32
CHUNK = 16
QPOS = 32
HIDDEN = -1e30
ALL = ("pipe", "y", "z", "core")
BF16 = jnp.bfloat16
F32 = jnp.float32


def column(row):
    return jnp.transpose(jnp.broadcast_to(row, (ROWS, ROWS)))


def order_matrix(times_row):
    across = jnp.broadcast_to(times_row, (ROWS, ROWS))
    down = jnp.transpose(across)
    i = lax.broadcasted_iota(jnp.int32, (ROWS, ROWS), 0)
    j = lax.broadcasted_iota(jnp.int32, (ROWS, ROWS), 1)
    before = jnp.where((down < across) | ((down == across) & (i < j)), 1.0, 0.0)
    rank = jnp.sum(before, axis=0, keepdims=True)
    return jnp.where(i.astype(F32) == rank, 1.0, 0.0)


def pair_columns(rows, pair, swap):
    low = rows[:, pair * HEAD_DIM : (pair + 1) * HEAD_DIM]
    high = rows[:, D // 2 + pair * HEAD_DIM : D // 2 + (pair + 1) * HEAD_DIM]
    return jnp.concatenate([high, low] if swap else [low, high], axis=1)


def pack_acts_kernel(times_ref, acts_ref, queries_ref, acts_out, queries_out):
    order = order_matrix(times_ref[0:1, :])
    low_order = order.astype(BF16)
    times = jnp.sum(order * column(times_ref[0:1, :]).T, axis=1, keepdims=True)
    times_row = jnp.transpose(jnp.broadcast_to(times, (ROWS, ROWS)))[0:16, :].astype(BF16)
    for source, target in ((acts_ref, acts_out), (queries_ref, queries_out)):
        ordered = jnp.dot(low_order, source[...], preferred_element_type=F32)
        for pair in range(RING):
            target[pair, 0:ROWS, :] = pair_columns(ordered, pair, False).astype(BF16)
    for pair in range(RING):
        acts_out[pair, ROWS : ROWS + 16, :] = times_row


def pack_grad_kernel(times_ref, grad_ref, grad_out):
    low_order = order_matrix(times_ref[0:1, :]).astype(BF16)
    ordered = jnp.dot(low_order, grad_ref[...], preferred_element_type=F32)
    for pair in range(RING):
        grad_out[pair] = pair_columns(ordered, pair, True).astype(BF16)


def unpack_kernel(times_ref, parts_ref, conv_ref, out_ref):
    low_order = order_matrix(times_ref[0:1, :]).astype(BF16)
    for pair in range(0, RING, 2):
        spans = []
        for one in (pair, pair + 1):
            spans.append(
                lax.dot_general(
                    low_order, parts_ref[one], (((0,), (0,)), ((), ())), preferred_element_type=F32
                )
            )
        low = jnp.concatenate([spans[0][:, :HEAD_DIM], spans[1][:, :HEAD_DIM]], axis=1)
        high = jnp.concatenate([spans[0][:, HEAD_DIM:], spans[1][:, HEAD_DIM:]], axis=1)
        at = pair * HEAD_DIM
        for start, block in ((at, low), (D // 2 + at, high)):
            span = slice(start, start + 2 * HEAD_DIM)
            out_ref[:, span] = (conv_ref[:, span] + block).astype(BF16)


def attention_kernel(
    acts_a, acts_b, acts_c, acts_d, queries_ref, grads_ref, gains_ref,
    near_ref, far_ref,
    keys, values, biases, scores, exps, key_acc, value_acc,
):
    key_gain = gains_ref[0:1, :]
    value_gain = gains_ref[1:2, :]
    lane = lax.broadcasted_iota(jnp.int32, (ROWS, PAIR), 1)
    lane_times = lane.astype(F32)
    key_acc[...] = jnp.zeros_like(key_acc)
    value_acc[...] = jnp.zeros_like(value_acc)
    firsts = None
    for group, acts in enumerate((acts_a, acts_b, acts_c, acts_d)):
        for source in range(RING):
            block = group * RING + source
            rows = acts[source, 0:ROWS, :].astype(F32)
            times_row = acts[source, ROWS : ROWS + 16, :].astype(F32)[0:1, :]
            firsts = times_row if firsts is None else jnp.minimum(firsts, times_row)
            times = column(times_row)
            keys[block, :, 0:PAIR] = (rows * key_gain).astype(BF16)
            keys[block, :, PAIR : 2 * PAIR] = jnp.where(lane_times == times, 1.0, 0.0).astype(BF16)
            values[block] = (rows * value_gain).astype(BF16)
            if group == 0:
                biases[source] = jnp.where(lane_times > times, HIDDEN, 0.0).astype(BF16)
                lasts = times_row if source == 0 else jnp.maximum(lasts, times_row)

    blocks = 4 * RING
    height = blocks * CHUNK
    width = RING * QPOS
    pos = lax.broadcasted_iota(jnp.int32, (1, ROWS), 1)
    upper = lax.broadcasted_iota(jnp.int32, (width, PAIR), 1) >= HEAD_DIM

    for q in range(ROWS // QPOS):
        latest = jnp.max(jnp.where(pos == (q + 1) * QPOS - 1, lasts, -1.0))
        starts = (firsts <= latest) & (pos % CHUNK == 0)
        visible = jnp.sum(jnp.where(starts, 1, 0))
        at = q * QPOS
        q_rows = queries_ref[:, at : at + QPOS, :].reshape(width, PAIR)
        g_rows = grads_ref[:, at : at + QPOS, :].reshape(width, PAIR)
        bias = biases[:, at : at + QPOS, :].reshape(width, PAIR)
        q_rows = q_rows.astype(F32) * HEAD_DIM**-0.5
        g_rows = g_rows.astype(F32)
        for head in range(2):
            own = upper if head else ~upper
            other = ~upper if head else upper
            q_head = jnp.where(own, q_rows, 0.0)
            g_head = jnp.where(other, g_rows, 0.0)
            q_low = jnp.concatenate([q_head.astype(BF16), bias], axis=1)
            g_low = g_head.astype(BF16)

            def find_max(c, top):
                rows = keys[:, pl.ds(pl.multiple_of(c * CHUNK, CHUNK), CHUNK), :].reshape(height, 2 * PAIR)
                s = lax.dot_general(rows, q_low, (((1,), (1,)), ((), ())), preferred_element_type=F32)
                scores[c] = s
                return jnp.maximum(top, jnp.max(s.reshape(height // 8, 8, width), axis=0))

            top = lax.fori_loop(0, visible, find_max, jnp.full((8, width), -jnp.inf, F32))
            top = jnp.max(top, axis=0, keepdims=True)

            def find_sums(c, sums):
                total, weighted = sums
                rows = values[:, pl.ds(pl.multiple_of(c * CHUNK, CHUNK), CHUNK), :].reshape(height, PAIR)
                dp = lax.dot_general(rows, g_low, (((1,), (1,)), ((), ())), preferred_element_type=F32)
                e = jnp.exp(scores[c] - top)
                exps[c] = e.astype(BF16)
                scores[c] = dp
                total = total + jnp.sum(e.reshape(height // 8, 8, width), axis=0)
                weighted = weighted + jnp.sum((e * dp).reshape(height // 8, 8, width), axis=0)
                return total, weighted

            zero = jnp.zeros((8, width), F32)
            total, weighted = lax.fori_loop(0, visible, find_sums, (zero, zero))
            inverse = 1.0 / jnp.sum(total, axis=0, keepdims=True)
            delta = jnp.sum(weighted, axis=0, keepdims=True) * inverse
            scale = jnp.concatenate(
                [column(inverse[:, k * ROWS : (k + 1) * ROWS]) for k in range(width // ROWS)], axis=0
            )
            q_scaled = (q_head * scale).astype(BF16)
            g_scaled = (g_head * scale).astype(BF16)

            def add_up(c, carry):
                span = pl.ds(pl.multiple_of(c * CHUNK, CHUNK), CHUNK)
                e = exps[c]
                ds = (e.astype(F32) * (scores[c] - delta)).astype(BF16)
                dv = jnp.dot(e, g_scaled, preferred_element_type=F32)
                dk = jnp.dot(ds, q_scaled, preferred_element_type=F32)
                value_acc[:, span, :] += dv.reshape(blocks, CHUNK, PAIR)
                key_acc[:, span, :] += dk.reshape(blocks, CHUNK, PAIR)
                return carry

            lax.fori_loop(0, visible, add_up, 0)

    for block in range(blocks):
        out = (key_acc[block] * key_gain + value_acc[block] * value_gain).astype(BF16)
        if block < 2 * RING:
            near_ref[block] = out
        else:
            far_ref[block - 2 * RING] = out


def in_vmem(count):
    return [pl.BlockSpec(memory_space=pltpu.VMEM)] * count


def pack_acts(times_row, acts, queries):
    return pl.pallas_call(
        pack_acts_kernel,
        out_shape=(
            jax.ShapeDtypeStruct((RING, ROWS + 16, PAIR), BF16),
            jax.ShapeDtypeStruct((RING, ROWS, PAIR), BF16),
        ),
        in_specs=in_vmem(3),
        out_specs=tuple(in_vmem(2)),
        cost_estimate=pl.CostEstimate(flops=2 * ROWS * ROWS * 2 * D, bytes_accessed=8 * ROWS * D, transcendentals=0),
    )(times_row, acts, queries)


def pack_grad(times_row, grad):
    return pl.pallas_call(
        pack_grad_kernel,
        out_shape=jax.ShapeDtypeStruct((RING, ROWS, PAIR), BF16),
        in_specs=in_vmem(2),
        out_specs=in_vmem(1)[0],
        cost_estimate=pl.CostEstimate(flops=2 * ROWS * ROWS * D, bytes_accessed=4 * ROWS * D, transcendentals=0),
    )(times_row, grad)


def unpack(times_row, parts, conv):
    return pl.pallas_call(
        unpack_kernel,
        out_shape=jax.ShapeDtypeStruct((ROWS, D), BF16),
        in_specs=in_vmem(3),
        out_specs=in_vmem(1)[0],
        cost_estimate=pl.CostEstimate(flops=2 * ROWS * ROWS * D, bytes_accessed=8 * ROWS * D, transcendentals=0),
    )(times_row, parts, conv)


def attention(acts, queries, grads, gains):
    chunks = ROWS // CHUNK
    height = 4 * RING * CHUNK
    width = RING * QPOS
    tokens = 4 * RING * ROWS
    return pl.pallas_call(
        attention_kernel,
        out_shape=(jax.ShapeDtypeStruct((2 * RING, ROWS, PAIR), BF16),) * 2,
        in_specs=in_vmem(7),
        out_specs=tuple(in_vmem(2)),
        scratch_shapes=[
            pltpu.VMEM((4 * RING, ROWS, 2 * PAIR), BF16),
            pltpu.VMEM((4 * RING, ROWS, PAIR), BF16),
            pltpu.VMEM((RING, ROWS, PAIR), BF16),
            pltpu.VMEM((chunks, height, width), F32),
            pltpu.VMEM((chunks, height, width), BF16),
            pltpu.VMEM((4 * RING, ROWS, PAIR), F32),
            pltpu.VMEM((4 * RING, ROWS, PAIR), F32),
        ],
        compiler_params=pltpu.CompilerParams(vmem_limit_bytes=40 * 1024 * 1024),
        cost_estimate=pl.CostEstimate(
            flops=2 * 4 * 2 * RING * ROWS * tokens * PAIR, bytes_accessed=4 * tokens * PAIR, transcendentals=2 * RING * ROWS * tokens
        ),
    )(*acts, queries, grads, gains)


def conv_backward(extended, weight, row_count):
    planes = row_count // (GY * GZ)
    grid_field = extended.reshape(planes + 2, GY, GZ, FIELDS, CHANNELS)
    padded = jnp.pad(grid_field, ((0, 0), (1, 1), (1, 1), (0, 0), (0, 0)))
    windows = []
    for shift_x in (-1, 0, 1):
        for shift_y in (-1, 0, 1):
            for shift_z in (-1, 0, 1):
                windows.append(
                    padded[
                        1 - shift_x : 1 - shift_x + planes,
                        1 - shift_y : 1 - shift_y + GY,
                        1 - shift_z : 1 - shift_z + GZ,
                    ]
                )
    stacked = jnp.stack(windows, axis=4).reshape(row_count * FIELDS, 27 * CHANNELS)
    matrix = jnp.transpose(weight, (0, 2, 1)).reshape(27 * CHANNELS, CHANNELS)
    return jnp.dot(stacked, matrix, preferred_element_type=F32).reshape(row_count, D)


def swapped(value, axis):
    return lax.ppermute(value, axis, [(0, 1), (1, 0)])


def exchanged(value):
    return lax.all_to_all(value, "z", split_axis=0, concat_axis=0, tiled=True)


def pair_gains(gain, pair):
    low = lax.dynamic_slice_in_dim(gain, pair * HEAD_DIM, HEAD_DIM, 1)
    high = lax.dynamic_slice_in_dim(gain, D // 2 + pair * HEAD_DIM, HEAD_DIM, 1)
    return jnp.concatenate([low, high], axis=1)


def on_device(
    sections, blocks, stored_acts, queries, patch_times, key_gain, value_gain, conv_weight, prior_grad, loss_grad
):
    times_row = patch_times.astype(F32)
    section = lax.axis_index("pipe")
    pair = lax.axis_index("z")
    sent = jnp.where(section == 0, loss_grad, prior_grad[0])
    edge = GY * GZ

    def from_next(value, step):
        perm = []
        for s in range(sections):
            for b in range(blocks):
                if 0 <= b + step < blocks:
                    perm.append((s * blocks + b, (s - 1) % sections * blocks + b + step))
        return lax.ppermute(value, ALL, perm)

    incoming = from_next(sent, 0)
    low = from_next(sent[ROWS - edge :], 1)
    high = from_next(sent[:edge], -1)

    acts_out, queries_out = pack_acts(times_row, stored_acts[0], queries[0])
    own = exchanged(acts_out)
    query_rows = exchanged(queries_out)
    grad_rows = exchanged(pack_grad(times_row, incoming))
    across = swapped(own, "y")
    own_core = swapped(own, "core")
    across_core = swapped(across, "core")

    extended = jnp.concatenate([low, incoming, high], axis=0)
    conv_part = conv_backward(extended, conv_weight[0], ROWS)

    gains = jnp.concatenate([pair_gains(key_gain, pair), pair_gains(value_gain, pair), jnp.zeros((6, PAIR), F32)], axis=0)
    near, far = attention((own, across, own_core, across_core), query_rows, grad_rows, gains)
    near = near.astype(F32) + swapped(far, "core").astype(F32)
    mine = near[:RING] + swapped(near[RING:].astype(BF16), "y").astype(F32)
    parts = exchanged(mine.astype(BF16))
    return unpack(times_row, parts, conv_part)[None]


def solution(mesh):
    sections, blocks = mesh.devices.shape
    fine = Mesh(mesh.devices.reshape(sections, 2, RING, 2), ALL)
    ctx = ("y", "z", "core")
    in_specs = (
        P("pipe", ctx, None),
        P("pipe", ctx, None),
        P("pipe", ctx),
        P("pipe", None),
        P("pipe", None),
        P("pipe", None, None, None),
        P("pipe", ctx, None),
        P(ctx, None),
    )
    return jax.shard_map(
        functools.partial(on_device, sections, blocks),
        mesh=fine,
        in_specs=in_specs,
        out_specs=P("pipe", ctx, None),
        check_vma=False,
    )
```

```python
import functools

import jax
import jax.numpy as jnp
from jax import lax
from jax.experimental import pallas as pl
from jax.experimental.pallas import tpu as pltpu
from jax.sharding import Mesh, PartitionSpec as P

HEADS = 16
HEAD_DIM = 64
CHANNELS = 128
GY = 8
GZ = 8
D = 1024
FIELDS = 8
ROWS = 128
PAIR = 128
RING = 8
NOTES = 16
CHUNK = 32
QPOS = 32
HIDDEN = -1e30
ALL = ("pipe", "y", "z", "core")
BF16 = jnp.bfloat16
F32 = jnp.float32


def column(row):
    return jnp.transpose(jnp.broadcast_to(row, (ROWS, ROWS)))


def order_matrix(times_row):
    across = jnp.broadcast_to(times_row, (ROWS, ROWS))
    down = jnp.transpose(across)
    i = lax.broadcasted_iota(jnp.int32, (ROWS, ROWS), 0)
    j = lax.broadcasted_iota(jnp.int32, (ROWS, ROWS), 1)
    before = jnp.where((down < across) | ((down == across) & (i < j)), 1.0, 0.0)
    rank = jnp.sum(before, axis=0, keepdims=True)
    return jnp.where(i.astype(F32) == rank, 1.0, 0.0)


def pair_columns(rows, pair, swap):
    low = rows[:, pair * HEAD_DIM : (pair + 1) * HEAD_DIM]
    high = rows[:, D // 2 + pair * HEAD_DIM : D // 2 + (pair + 1) * HEAD_DIM]
    return jnp.concatenate([high, low] if swap else [low, high], axis=1)


def pack_kernel(place_ref, times_ref, acts_ref, queries_ref, prior_ref, loss_ref, rows_out):
    section = place_ref[1]
    times_row = times_ref[0:1, :].astype(F32)
    order = order_matrix(times_row)
    low_order = order.astype(BF16)
    sorted_times = jnp.sum(order * jnp.broadcast_to(times_row, (ROWS, ROWS)), axis=1, keepdims=True)
    sorted_row = jnp.transpose(jnp.broadcast_to(sorted_times, (ROWS, ROWS)))[0:8, :]
    notes = jnp.concatenate([sorted_row, jnp.broadcast_to(times_row, (8, ROWS))], axis=0).astype(BF16)
    for source, first in ((acts_ref, 0), (queries_ref, ROWS + NOTES)):
        ordered = jnp.dot(low_order, source[...], preferred_element_type=F32)
        for pair in range(RING):
            rows_out[pair, first : first + ROWS, :] = pair_columns(ordered, pair, False).astype(BF16)
    for pair in range(RING):
        rows_out[pair, ROWS : ROWS + NOTES, :] = notes
    sent = jnp.where(section == 0, loss_ref[...].astype(F32), prior_ref[...].astype(F32))
    for pair in range(RING):
        rows_out[pair, 2 * ROWS + NOTES :, :] = pair_columns(sent, pair, True).astype(BF16)


def unpack_kernel(times_ref, parts_ref, conv_ref, out_ref):
    low_order = order_matrix(times_ref[0:1, :].astype(F32)).astype(BF16)
    for pair in range(0, RING, 2):
        spans = []
        for one in (pair, pair + 1):
            halves = [
                lax.dot_general(
                    low_order, parts_ref[half * RING + one], (((0,), (0,)), ((), ())), preferred_element_type=F32
                )
                for half in range(2)
            ]
            spans.append(halves[0] + halves[1])
        low = jnp.concatenate([spans[0][:, :HEAD_DIM], spans[1][:, :HEAD_DIM]], axis=1)
        high = jnp.concatenate([spans[0][:, HEAD_DIM:], spans[1][:, HEAD_DIM:]], axis=1)
        at = pair * HEAD_DIM
        for start, block in ((at, low), (D // 2 + at, high)):
            span = slice(start, start + 2 * HEAD_DIM)
            out_ref[:, span] = (conv_ref[:, span] + block).astype(BF16)


def attention_kernel(
    place_ref, acts_a, acts_b, acts_c, acts_d, *rest
):
    grads_in, gains_ref, near_ref, far_ref = rest[:4]
    (
        grads, keys, values, biases, scores_a, scores_b, slopes_a, slopes_b, key_acc, value_acc,
    ) = rest[4:]
    lane_y = place_ref[2]
    key_gain = gains_ref[0:1, :]
    value_gain = gains_ref[1:2, :]
    lane = lax.broadcasted_iota(jnp.int32, (ROWS, PAIR), 1)
    lane_times = lane.astype(F32)
    key_acc[...] = jnp.zeros_like(key_acc)
    value_acc[...] = jnp.zeros_like(value_acc)
    firsts = None
    for group, acts in enumerate((acts_a, acts_b, acts_c, acts_d)):
        for source in range(RING):
            block = group * RING + source
            rows = acts[source, 0:ROWS, :].astype(F32)
            times_row = acts[source, ROWS : ROWS + NOTES, :].astype(F32)[0:1, :]
            firsts = times_row if firsts is None else jnp.minimum(firsts, times_row)
            times = column(times_row)
            keys[block, :, 0:PAIR] = (rows * key_gain).astype(BF16)
            keys[block, :, PAIR : 2 * PAIR] = jnp.where(lane_times == times, 1.0, 0.0).astype(BF16)
            values[block] = (rows * value_gain).astype(BF16)
            if group == 0:
                biases[source] = jnp.where(lane_times > times, HIDDEN, 0.0).astype(BF16)
                lasts = times_row if source == 0 else jnp.maximum(lasts, times_row)

    for source in range(RING):
        raw_row = acts_a[source, ROWS : ROWS + NOTES, :].astype(F32)[8:9, :]
        low_order = order_matrix(raw_row).astype(BF16)
        grads[source] = jnp.dot(low_order, grads_in[source], preferred_element_type=F32).astype(BF16)

    blocks = 4 * RING
    height = blocks * CHUNK
    width = RING * QPOS
    pos = lax.broadcasted_iota(jnp.int32, (1, ROWS), 1)
    upper = lax.broadcasted_iota(jnp.int32, (width, PAIR), 1) >= HEAD_DIM

    both = 2 * width
    nt = (((1,), (1,)), ((), ()))

    def folded(rows, combine):
        return combine(rows.reshape(height // 8, 8, both), axis=0)

    def first_pass(c, stats, q_low, g_low, scores, slopes):
        top, total, weighted = stats
        span = pl.ds(pl.multiple_of(c * CHUNK, CHUNK), CHUNK)
        s = lax.dot_general(keys[:, span, :].reshape(height, 2 * PAIR), q_low, nt, preferred_element_type=F32)
        scores[c] = s
        dp = lax.dot_general(values[:, span, :].reshape(height, PAIR), g_low, nt, preferred_element_type=F32)
        slopes[c] = dp
        new_top = jnp.maximum(top, jnp.max(folded(s, jnp.max), axis=0, keepdims=True))
        e = jnp.exp(s - new_top)
        factor = jnp.exp(top - new_top)
        return new_top, total * factor + folded(e, jnp.sum), weighted * factor + folded(e * dp, jnp.sum)

    def second_pass(c, shift, delta, q_low, g_low, scores, slopes):
        span = pl.ds(pl.multiple_of(c * CHUNK, CHUNK), CHUNK)
        p = jnp.exp(scores[c] - shift)
        ds = (p * (slopes[c] - delta)).astype(BF16)
        dv = jnp.dot(p.astype(BF16), g_low, preferred_element_type=F32)
        dk = jnp.dot(ds, q_low[:, :PAIR], preferred_element_type=F32)
        value_acc[:, span, :] += dv.reshape(blocks, CHUNK, PAIR)
        key_acc[:, span, :] += dk.reshape(blocks, CHUNK, PAIR)

    earlier = None
    seen = 0
    for q in range(ROWS // QPOS):
        latest = jnp.max(jnp.where(pos == (q + 1) * QPOS - 1, lasts, -1.0))
        starts = (firsts <= latest) & (pos % CHUNK == 0)
        visible = jnp.sum(jnp.where(starts, 1, 0))
        at = q * QPOS
        q_rows = acts_a[:, ROWS + NOTES + at : ROWS + NOTES + at + QPOS, :].reshape(width, PAIR).astype(F32) * HEAD_DIM**-0.5
        g_rows = grads[:, at : at + QPOS, :].reshape(width, PAIR).astype(F32)
        bias = biases[:, at : at + QPOS, :].reshape(width, PAIR)
        q_both = jnp.concatenate([jnp.where(upper, 0.0, q_rows), jnp.where(upper, q_rows, 0.0)], axis=0)
        g_both = jnp.concatenate([jnp.where(upper, g_rows, 0.0), jnp.where(upper, 0.0, g_rows)], axis=0)
        q_low = jnp.concatenate([q_both.astype(BF16), jnp.concatenate([bias, bias], axis=0)], axis=1)
        g_low = g_both.astype(BF16)
        buffers = (scores_a, slopes_a) if q % 2 == 0 else (scores_b, slopes_b)

        def merged(c, stats):
            second_pass(c, *earlier)
            return first_pass(c, stats, q_low, g_low, *buffers)

        def alone(c, stats):
            return first_pass(c, stats, q_low, g_low, *buffers)

        zero = jnp.zeros((8, both), F32)
        stats = (jnp.full((1, both), -1e30, F32), zero, zero)
        if earlier is not None:
            stats = lax.fori_loop(0, seen, merged, stats)
        stats = lax.fori_loop(seen, visible, alone, stats)
        top, total, weighted = stats
        total = jnp.sum(total, axis=0, keepdims=True)
        delta = jnp.sum(weighted, axis=0, keepdims=True) / total
        earlier = (top + jnp.log(total), delta, q_low, g_low, *buffers)
        seen = visible

    def last(c, carry):
        second_pass(c, *earlier)
        return carry

    lax.fori_loop(0, seen, last, 0)

    for block in range(blocks):
        out = (key_acc[block] * key_gain + value_acc[block] * value_gain).astype(BF16)
        side = block // RING % 2
        target = near_ref if block < 2 * RING else far_ref
        target[(lane_y if side == 0 else 1 - lane_y) * RING + block % RING] = out


def in_vmem(count):
    return [pl.BlockSpec(memory_space=pltpu.VMEM)] * count


def pack(place, times, acts, queries, prior, loss):
    smem = pl.BlockSpec(memory_space=pltpu.SMEM)
    return pl.pallas_call(
        pack_kernel,
        out_shape=jax.ShapeDtypeStruct((RING, 3 * ROWS + NOTES, PAIR), BF16),
        in_specs=[smem, *in_vmem(5)],
        out_specs=in_vmem(1)[0],
        cost_estimate=pl.CostEstimate(flops=2 * ROWS * ROWS * 2 * D, bytes_accessed=14 * ROWS * D, transcendentals=0),
    )(place, times, acts, queries, prior, loss)


def unpack(times_row, parts, conv):
    return pl.pallas_call(
        unpack_kernel,
        out_shape=jax.ShapeDtypeStruct((ROWS, D), BF16),
        in_specs=in_vmem(3),
        out_specs=in_vmem(1)[0],
        cost_estimate=pl.CostEstimate(flops=2 * ROWS * ROWS * D, bytes_accessed=8 * ROWS * D, transcendentals=0),
    )(times_row, parts, conv)


def attention(place, acts, grads, gains):
    chunks = ROWS // CHUNK
    height = 4 * RING * CHUNK
    width = RING * QPOS
    tokens = 4 * RING * ROWS
    return pl.pallas_call(
        attention_kernel,
        out_shape=(jax.ShapeDtypeStruct((2 * RING, ROWS, PAIR), BF16),) * 2,
        in_specs=[pl.BlockSpec(memory_space=pltpu.SMEM), *in_vmem(6)],
        out_specs=tuple(in_vmem(2)),
        scratch_shapes=[
            pltpu.VMEM((RING, ROWS, PAIR), BF16),
            pltpu.VMEM((4 * RING, ROWS, 2 * PAIR), BF16),
            pltpu.VMEM((4 * RING, ROWS, PAIR), BF16),
            pltpu.VMEM((RING, ROWS, PAIR), BF16),
            pltpu.VMEM((chunks, height, 2 * width), F32),
            pltpu.VMEM((chunks, height, 2 * width), F32),
            pltpu.VMEM((chunks, height, 2 * width), F32),
            pltpu.VMEM((chunks, height, 2 * width), F32),
            pltpu.VMEM((4 * RING, ROWS, PAIR), F32),
            pltpu.VMEM((4 * RING, ROWS, PAIR), F32),
        ],
        compiler_params=pltpu.CompilerParams(vmem_limit_bytes=56 * 1024 * 1024),
        cost_estimate=pl.CostEstimate(
            flops=2 * 4 * 2 * RING * ROWS * tokens * PAIR, bytes_accessed=4 * tokens * PAIR, transcendentals=2 * RING * ROWS * tokens
        ),
    )(place, *acts, grads, gains)


def conv_kernel(low_ref, rows_ref, high_ref, weight_ref, out_ref, padded):
    edge = GY * GZ
    planes = ROWS // edge + 2
    z = lax.broadcasted_iota(jnp.int32, (edge, CHANNELS), 0) % GZ
    empty = jnp.zeros((planes, GZ, 3 * CHANNELS), F32)
    for field in range(FIELDS):
        span = slice(field * CHANNELS, (field + 1) * CHANNELS)
        padded[field, :, 0] = empty
        padded[field, :, GY + 1] = empty
        for plane in range(planes):
            if plane == 0:
                rows = low_ref[:, span]
            elif plane == planes - 1:
                rows = high_ref[:, span]
            else:
                rows = rows_ref[(plane - 1) * edge : plane * edge, span]
            rows = rows.astype(F32)
            after = jnp.where(z == GZ - 1, 0.0, jnp.concatenate([rows[1:], rows[:1]], axis=0))
            before = jnp.where(z == 0, 0.0, jnp.concatenate([rows[-1:], rows[:-1]], axis=0))
            wide = jnp.concatenate([after, rows, before], axis=1)
            padded[field, plane, 1 : GY + 1] = wide.reshape(GY, GZ, 3 * CHANNELS)
    total = None
    for shift_x in (-1, 0, 1):
        for shift_y in (-1, 0, 1):
            first = 9 * (shift_x + 1) + 3 * (shift_y + 1)
            matrix = jnp.concatenate([weight_ref[first + k] for k in range(3)], axis=1)
            window = padded[:, 1 - shift_x : planes - 1 - shift_x, 1 - shift_y : 1 - shift_y + GY]
            part = lax.dot_general(
                window.astype(BF16).reshape(FIELDS * ROWS, 3 * CHANNELS),
                matrix,
                (((1,), (1,)), ((), ())),
                preferred_element_type=F32,
            )
            total = part if total is None else total + part
    for field in range(FIELDS):
        out_ref[:, field * CHANNELS : (field + 1) * CHANNELS] = total[field * ROWS : (field + 1) * ROWS]


def conv_backward(low, rows, high, weight):
    planes = ROWS // (GY * GZ) + 2
    return pl.pallas_call(
        conv_kernel,
        out_shape=jax.ShapeDtypeStruct((ROWS, D), F32),
        in_specs=in_vmem(4),
        out_specs=in_vmem(1)[0],
        scratch_shapes=[pltpu.VMEM((FIELDS, planes, GY + 2, GZ, 3 * CHANNELS), F32)],
        compiler_params=pltpu.CompilerParams(vmem_limit_bytes=24 * 1024 * 1024),
        cost_estimate=pl.CostEstimate(flops=2 * 27 * ROWS * D * CHANNELS, bytes_accessed=8 * ROWS * D, transcendentals=0),
    )(low, rows, high, weight)


def swapped(value, axis):
    return lax.ppermute(value, axis, [(0, 1), (1, 0)])


def exchanged(value, axis):
    return lax.all_to_all(value, axis, split_axis=0, concat_axis=0, tiled=True)


def pair_gains(gain, pair):
    low = lax.dynamic_slice_in_dim(gain, pair * HEAD_DIM, HEAD_DIM, 1)
    high = lax.dynamic_slice_in_dim(gain, D // 2 + pair * HEAD_DIM, HEAD_DIM, 1)
    return jnp.concatenate([low, high], axis=1)


def on_device(
    sections, blocks, stored_acts, queries, patch_times, key_gain, value_gain, conv_weight, prior_grad, loss_grad
):
    section, side, ring = lax.axis_index("pipe"), lax.axis_index("y"), lax.axis_index("z")
    place = jnp.stack([ring, section, side]).astype(jnp.int32)

    def from_next(value, step):
        perm = []
        for s in range(sections):
            for b in range(blocks):
                if 0 <= b + step < blocks:
                    perm.append((s * blocks + b, (s - 1) % sections * blocks + b + step))
        return lax.ppermute(value, ALL, perm)

    rows_out = pack(place, patch_times, stored_acts[0], queries[0], prior_grad[0], loss_grad)
    own = exchanged(rows_out, "z")
    grads = from_next(own[:, 2 * ROWS + NOTES :], 0)
    own_acts = own[:, : ROWS + NOTES]
    across = swapped(own_acts, "y")
    own_core = swapped(own_acts, "core")
    across_core = swapped(across, "core")

    gains = jnp.concatenate([pair_gains(key_gain, ring), pair_gains(value_gain, ring), jnp.zeros((6, PAIR), F32)], axis=0)
    near, far = attention(place, (own, across, own_core, across_core), grads, gains)

    near, edges = lax.optimization_barrier((near, jnp.where(section == 0, loss_grad, prior_grad[0])))
    incoming = from_next(edges, 0)
    low = from_next(edges[ROWS - GY * GZ :], 1)
    high = from_next(edges[: GY * GZ], -1)
    conv_part = conv_backward(low, incoming, high, conv_weight[0])

    mine = (near.astype(F32) + swapped(far, "core").astype(F32)).astype(BF16)
    parts = exchanged(mine, ("y", "z"))
    return unpack(patch_times, parts, conv_part)[None]


def solution(mesh):
    sections, blocks = mesh.devices.shape
    fine = Mesh(mesh.devices.reshape(sections, 2, RING, 2), ALL)
    ctx = ("y", "z", "core")
    in_specs = (
        P("pipe", ctx, None),
        P("pipe", ctx, None),
        P("pipe", ctx),
        P("pipe", None),
        P("pipe", None),
        P("pipe", None, None, None),
        P("pipe", ctx, None),
        P(ctx, None),
    )
    return jax.shard_map(
        functools.partial(on_device, sections, blocks),
        mesh=fine,
        in_specs=in_specs,
        out_specs=P("pipe", ctx, None),
        check_vma=False,
    )
```
